32 devices in a mesh: gx: 4 (over y, x), gy: 4 (over z), gz: 2 (over core).
Axes of the slice: x: 2, y: 2, z: 4, core: 2. Of those that a mesh axis runs over, the one named last changes fastest.
Arguments:
- positions: float32 [3, 32768], P(None, ('gx', 'gy', 'gz')), as said below
- polarizability: float32 [4, 2, 32768], P(None, None, ('gx', 'gy', 'gz')), may hold values from -0.5 to 1
- applied_field: float32 [4, 2, 3, 32768], P(None, None, None, ('gx', 'gy', 'gz')), may hold values from -6 to 6
- pair_codes: int32 [768], P(('gx', 'gy', 'gz')), may hold values from 0 to 1151
- pair_counts: int32 [32], P(('gx', 'gy', 'gz')), may hold values from 3 to 24, as said below
Outputs:
- dipoles: float32 [4, 2, 3, 32768], P(None, None, None, ('gx', 'gy', 'gz'))
The draws below stay inside these ranges and needn't reach their ends.
Inputs may be any that keep to these rules, and one draw needn't show every extreme that they name: `pair_codes`: each code is ((dx + 1) * 3 + (dy + 1)) * 2 * 8^2 + zt * 8^2 + target_block * 8 + source_block with dx, dy in -1..1, zt in 0..1 and blocks in 0..7; only the first pair_counts entries of a device's list are live. `pair_counts`: some device has 24 live entries in every draw. `positions`: x and y lie in [0, 4) within the owner's slab cell; z lies in [2 z_half, 2 z_half + 2) for the owner's depth half.
All inputs are finite; a program needn't handle non-finite values.
Results may differ from the reference program's by a relative error of at most 0.0003.
Values sent between devices are 32-bit elements; how exact they have to be, the bound alone decides.
A program may use at most 64 MiB of HBM per device.

```python
import math
import jax
import jax.numpy as jnp
from jax import lax

BLOCK = 128
BLOCKS = 8
FREQS = 4
ITERS = 4
PAIRS = 24
PARTICLES = 32768
N_GX = 4
N_GY = 4
N_GZ = 2
DEVICES = 32


cell_width = 4.0


half_depth = 2.0


def draw_positions(key, part):
    count = BLOCKS * BLOCK * DEVICES
    uniform_draw = jax.random.uniform(key, (3, count), jnp.float32)
    owner_half = (jnp.arange(count, dtype=jnp.int32) // (BLOCKS * BLOCK) % N_GZ).astype(jnp.float32)
    plane = uniform_draw[:2] * cell_width
    across = (uniform_draw[2] + owner_half) * half_depth
    return jnp.concatenate([plane, across[None, :]], axis=0)


def draw_pair_counts(key, part):
    key_base, key_crowd, key_pick = jax.random.split(key, 3)
    base_counts = jax.random.randint(key_base, (DEVICES,), PAIRS // 8, PAIRS // 3 + 1)
    crowded = jax.random.randint(key_crowd, (DEVICES,), 0, 8) == 0
    chosen = jax.random.randint(key_pick, (), 0, DEVICES)
    crowded = crowded | (jnp.arange(DEVICES, dtype=jnp.int32) == chosen)
    return jnp.where(crowded, PAIRS, base_counts).astype(jnp.int32)


def touch_ends(drawn, key, low, top_value):
    extent = drawn.shape
    place = [jax.random.randint(jax.random.fold_in(key, axis), (), 0, extent[axis]) for axis in range(len(extent))]
    drawn = drawn.at[tuple(place)].set(low)
    longest = extent.index(max(extent))
    place[longest] = (place[longest] + 1) % extent[longest]
    return drawn.at[tuple(place)].set(top_value)


def block_scale(own_key, extent, cuts, smallest, top_value):
    factor_of = 1.0
    for axis_at, shards_of in cuts:
        steps = jax.random.uniform(jax.random.fold_in(jax.random.fold_in(own_key, 6), axis_at), (shards_of,), jnp.float32, smallest / len(cuts), top_value / len(cuts))
        factor_of = factor_of * jnp.repeat(jnp.exp(steps), extent[axis_at] // shards_of).reshape((-1,) + (1,) * (len(extent) - 1 - axis_at))
    return factor_of


def normal_values(own_key, shape, deviation, reach, cuts=(), kind=jnp.bfloat16):
    level = block_scale(own_key, shape, cuts, -0.22, 0.18) if cuts else 1.0
    values = jax.random.normal(own_key, shape, jnp.float32) * deviation * level
    return jnp.minimum(jnp.maximum(values, -reach), reach).astype(kind)


def setup_inputs(seed: int = 0) -> dict:
    seeds = jax.random.split(jax.random.key(seed), 6)
    return {
        "positions": draw_positions(jax.random.fold_in(seeds[5], 71), 0),
        "polarizability": jnp.clip(-0.5 + 1.5 * jax.random.uniform(seeds[1], (FREQS, 2, PARTICLES), jnp.float32) ** block_scale(seeds[1], (FREQS, 2, PARTICLES), ((2, 32),), -0.2, 0.2), -0.5, 1.0),
        "applied_field": normal_values(seeds[2], (FREQS, 2, 3, PARTICLES), 1.0, 6.0, ((3, 32),), jnp.float32),
        "pair_codes": touch_ends(jax.random.randint(seeds[3], (N_GX * N_GY * N_GZ * PAIRS,), 0, 18 * BLOCKS * BLOCKS), jax.random.fold_in(seeds[3], 1), 0, (18 * BLOCKS * BLOCKS) - 1).astype(jnp.int32),
        "pair_counts": draw_pair_counts(jax.random.fold_in(seeds[5], 71), 0),
    }


cell_width = 4.0
soften = 1.0
screen = 0.5
coupling = 0.8

def tensor_field(tgt_pos, src_pos, shift_x, shift_y, sources):
    disp_x = tgt_pos[0][:, None] - src_pos[0][None, :] + shift_x
    disp_y = tgt_pos[1][:, None] - src_pos[1][None, :] + shift_y
    disp_z = tgt_pos[2][:, None] - src_pos[2][None, :]
    dist_sq = disp_x * disp_x + disp_y * disp_y + disp_z * disp_z + soften * soften
    inv_dist = lax.rsqrt(dist_sq)
    distance = dist_sq * inv_dist
    screened = jax.scipy.special.erfc(screen * distance)
    gaussian = 2.0 * screen / math.sqrt(math.pi) * jnp.exp(-screen * screen * dist_sq)
    inv_sq = inv_dist * inv_dist
    b_term = screened * inv_sq * inv_dist + gaussian * inv_sq
    c_term = (3.0 * screened * inv_sq * inv_dist + gaussian * (2.0 * screen * screen + 3.0 * inv_sq)) * inv_sq
    disp_vec = jnp.stack([disp_x, disp_y, disp_z])
    tensor = c_term[None, :, None, :] * disp_vec[:, :, None, :] * jnp.transpose(disp_vec, (1, 0, 2))[None, :, :, :]
    tensor = tensor - jnp.eye(3, dtype=tensor.dtype)[:, None, :, None] * b_term[None, :, None, :]
    block_len = tgt_pos.shape[1]
    matrix = tensor.reshape(3 * block_len, 3 * block_len)
    flat_src = sources.reshape(-1, 3 * block_len)
    result = lax.dot_general(flat_src, matrix, (((1,), (1,)), ((), ())), precision=lax.Precision.HIGHEST, preferred_element_type=jnp.float32)
    return result.reshape(sources.shape)

def reference(positions, polarizability, applied_field, pair_codes, pair_counts):
    freqs = polarizability.shape[0]
    device_count = N_GX * N_GY * N_GZ
    block_count = BLOCKS * device_count
    pos_blocks = positions.reshape(3, block_count, BLOCK).transpose(1, 0, 2)
    alpha_blocks = polarizability.reshape(freqs, 2, block_count, BLOCK).transpose(2, 0, 1, 3)
    field_blocks = applied_field.reshape(freqs, 2, 3, block_count, BLOCK).transpose(3, 0, 1, 2, 4)
    a_re = alpha_blocks[:, :, 0][:, :, None]
    a_im = alpha_blocks[:, :, 1][:, :, None]

    def respond(field_re, field_im):
        return jnp.stack([a_re * field_re - a_im * field_im, a_re * field_im + a_im * field_re], axis=2)
    square = BLOCKS * BLOCKS

    def induced(dipoles):

        def per_device(total, device):
            slab_x = device // (N_GY * N_GZ)
            slab_y = device // N_GZ % N_GY
            depth = device % N_GZ
            pair_list = lax.dynamic_slice_in_dim(pair_codes, (device * PAIRS).astype(jnp.int32), PAIRS)
            pair_total = pair_counts[device]
            src_block = pair_list % BLOCKS
            tgt_block = pair_list // BLOCKS % BLOCKS
            depth_tgt = pair_list // square % 2
            step_y = pair_list // (2 * square) % 3 - 1
            step_x = pair_list // (6 * square) - 1
            src_index = (((slab_x + step_x) % N_GX * N_GY + slab_y) * N_GZ + depth) * BLOCKS + src_block
            tgt_index = ((slab_x * N_GY + (slab_y + step_y) % N_GY) * N_GZ + depth_tgt) * BLOCKS + tgt_block
            shift_x = -step_x.astype(jnp.float32) * cell_width
            shift_y = step_y.astype(jnp.float32) * cell_width
            contrib = jax.vmap(tensor_field)(pos_blocks[tgt_index], pos_blocks[src_index], shift_x, shift_y, dipoles[src_index])
            active = (jnp.arange(PAIRS, dtype=jnp.int32) < pair_total).astype(jnp.float32)
            return (total.at[tgt_index].add(contrib * active[:, None, None, None, None]), None)
        total, unused = lax.scan(per_device, jnp.zeros_like(dipoles), jnp.arange(device_count, dtype=jnp.int32))
        return total
    dipoles = respond(field_blocks[:, :, 0], field_blocks[:, :, 1])
    for sweep in range(ITERS):
        field = induced(dipoles)
        dipoles = respond(field_blocks[:, :, 0] + coupling * field[:, :, 0], field_blocks[:, :, 1] + coupling * field[:, :, 1])
    return dipoles.transpose(1, 2, 3, 0, 4).reshape(freqs, 2, 3, block_count * BLOCK)
```

```python
import functools
import math

import jax
import jax.numpy as jnp
from jax import lax
from jax.experimental import pallas as pl
from jax.experimental.pallas import tpu as pltpu
from jax.sharding import PartitionSpec as P

BLOCK = 128
ITERS = 4
UNROLL = 4

cell_width = 4.0
soften = 1.0
screen = 0.5
coupling = 0.8

CENTER = 0.54
SERIES = (
    0.806488610702616,
    0.7241185361715909,
    0.27511941992319955,
    -0.26086845400919295,
    0.2296813716405795,
    -0.17763507721765817,
    0.1043247007059023,
    -0.02452746718798479,
    -0.07547989643924369,
    0.2975431845822381,
    -0.5276853186117066,
    0.345520543574722,
)
MESH = pl.DeviceIdType.MESH


def split(value):
    high = value.astype(jnp.bfloat16)
    low = (value - high.astype(jnp.float32)).astype(jnp.bfloat16)
    return high, low


def kernel(
    sizes,
    codes_ref,
    count_ref,
    pos_ref,
    a1_ref,
    a2_ref,
    field_ref,
    out_ref,
    src_pos,
    tgt_pos,
    tensors,
    choose,
    chosen,
    sources,
    halves,
    contribs,
    partial,
    depth_in,
    carry_in,
    pos_send,
    pos_recv,
    x_send,
    x_recv,
    z_send,
    z_recv,
    y_send,
    y_recv,
):
    n_x, n_y, nblocks, pairs = sizes
    square = nblocks * nblocks
    rows = field_ref.shape[1]
    x = lax.axis_index("gx")
    y = lax.axis_index("gy")
    z = lax.axis_index("gz")
    x_up, x_down = lax.rem(x + 1, n_x), lax.rem(x + n_x - 1, n_x)
    y_up, y_down = lax.rem(y + 1, n_y), lax.rem(y + n_y - 1, n_y)
    other = 1 - z

    barrier = pltpu.get_barrier_semaphore()
    partners = (
        (x_up, y, z),
        (x_down, y, z),
        (x, y_up, z),
        (x, y_down, z),
        (x, y_up, other),
        (x, y_down, other),
        (x, y, other),
    )
    for partner in partners:
        pl.semaphore_signal(barrier, inc=1, device_id=partner, device_id_type=MESH)

    def respond(field, block):
        turned = jnp.concatenate([field[rows // 2 :], field[: rows // 2]], axis=0)
        return a1_ref[block] * field + a2_ref[block] * turned

    for block in range(nblocks):
        for k in range(3):
            lanes = pl.ds(k * BLOCK, BLOCK)
            sources[0, 1, block, :, lanes] = respond(field_ref[block, :, lanes], block)
    src_pos[1] = pos_ref[...]
    tgt_pos[1] = pos_ref[...]

    def send(src, dst, send_sem, recv_sem, device):
        return pltpu.make_async_remote_copy(
            src_ref=src,
            dst_ref=dst,
            send_sem=send_sem,
            recv_sem=recv_sem,
            device_id=device,
            device_id_type=MESH,
        )

    pl.semaphore_wait(barrier, len(partners))

    def x_copies(sweep):
        return (
            send(sources.at[sweep, 1], sources.at[sweep, 0], x_send.at[sweep, 0], x_recv.at[sweep, 0], (x_up, y, z)),
            send(sources.at[sweep, 1], sources.at[sweep, 2], x_send.at[sweep, 1], x_recv.at[sweep, 1], (x_down, y, z)),
        )

    pos_copies = (
        send(pos_ref, src_pos.at[0], pos_send.at[0], pos_recv.at[0], (x_up, y, z)),
        send(pos_ref, src_pos.at[2], pos_send.at[1], pos_recv.at[1], (x_down, y, z)),
        send(pos_ref, tgt_pos.at[0], pos_send.at[2], pos_recv.at[2], (x, y_up, z)),
        send(pos_ref, tgt_pos.at[2], pos_send.at[3], pos_recv.at[3], (x, y_down, z)),
        send(pos_ref, tgt_pos.at[3], pos_send.at[4], pos_recv.at[4], (x, y_up, other)),
        send(pos_ref, tgt_pos.at[5], pos_send.at[5], pos_recv.at[5], (x, y_down, other)),
        send(pos_ref, tgt_pos.at[4], pos_send.at[6], pos_recv.at[6], (x, y, other)),
    )
    for copy in pos_copies:
        copy.start()
    for copy in x_copies(0):
        copy.start()
    for copy in pos_copies:
        copy.wait()

    def decode(entry):
        code = codes_ref[entry]
        src_block = code % nblocks
        tgt_block = code // nblocks % nblocks
        depth_tgt = code // square % 2
        step_y = code // (2 * square) % 3
        step_x = code // (6 * square)
        turned_depth = (depth_tgt + z) % 2
        return src_block, tgt_block, turned_depth, step_y, step_x

    def build(entry, carried):
        src_block, tgt_block, depth, step_y, step_x = decode(entry)
        src = src_pos[step_x, src_block].T
        tgt = tgt_pos[depth * 3 + step_y, tgt_block]
        shift_x = (step_x - 1).astype(jnp.float32) * -cell_width
        shift_y = (step_y - 1).astype(jnp.float32) * cell_width
        disp = [
            tgt[0:1] - src[:, 0:1] + shift_x,
            tgt[1:2] - src[:, 1:2] + shift_y,
            tgt[2:3] - src[:, 2:3],
        ]
        dist_sq = disp[0] * disp[0] + disp[1] * disp[1] + disp[2] * disp[2] + soften * soften
        inv = lax.rsqrt(dist_sq)
        inv_sq = inv * inv
        offset = inv - CENTER
        series = jnp.full_like(offset, SERIES[-1])
        for term in SERIES[-2::-1]:
            series = series * offset + term
        scale = jnp.exp(-screen * screen * dist_sq) * inv_sq
        b_term = scale * series
        c_term = scale * (3.0 * inv_sq * series + 2.0 * screen * screen / math.sqrt(math.pi))
        for a in range(3):
            scaled = c_term * disp[a]
            for b in range(a, 3):
                value = scaled * disp[b]
                if a == b:
                    value = value - b_term
                high, low = split(value)
                for r, c in {(a, b), (b, a)}:
                    lanes = pl.ds(c * BLOCK, BLOCK)
                    tensors[entry, pl.ds(r * BLOCK, BLOCK), lanes] = high
                    tensors[entry, pl.ds((3 + r) * BLOCK, BLOCK), lanes] = low
        slot = (depth * 3 + step_y) * nblocks + tgt_block
        slot = jnp.where(entry < count_ref[0], slot, -1)
        shape = (rows, 6 * nblocks * rows)
        column = lax.broadcasted_iota(jnp.int32, shape, 1)
        row = lax.broadcasted_iota(jnp.int32, shape, 0)
        choose[pl.ds(entry * rows, rows), :] = jnp.where(column == slot * rows + row, 1.0, 0.0)
        return carried

    lax.fori_loop(0, pairs, build, 0)
    chosen[...] = choose[...].T.astype(jnp.bfloat16)

    def sweep_step(sweep, carried):
        copies = x_copies(sweep)
        for copy in copies:
            copy.wait()
        for step in range(3):
            for block in range(nblocks):
                high, low = split(sources[sweep, step, block])
                halves[step, block] = jnp.concatenate([high, low], axis=0)

        def pair_step(group, carried):
            for member in range(UNROLL):
                entry = group * UNROLL + member
                src_block, _, _, _, step_x = decode(entry)
                both = halves[step_x, src_block]
                both = jnp.concatenate([both, both], axis=1)
                result = jnp.dot(both, tensors[entry], preferred_element_type=jnp.float32)
                contribs[pl.ds(entry * rows, rows), :] = result[:rows] + result[rows:]
            return carried

        lax.fori_loop(0, pairs // UNROLL, pair_step, 0)
        high, low = split(contribs[...])
        merged = jnp.dot(chosen[...], high, preferred_element_type=jnp.float32) + jnp.dot(
            chosen[...], low, preferred_element_type=jnp.float32
        )
        partial[sweep] = merged.reshape(6, nblocks, rows, 3 * BLOCK)

        z_copies = [
            send(
                partial.at[sweep, 3 + step],
                depth_in.at[sweep, step],
                z_send.at[sweep, step],
                z_recv.at[sweep, step],
                (x, y, other),
            )
            for step in range(3)
        ]
        y_copies = [
            send(partial.at[sweep, 0], carry_in.at[sweep, 0], y_send.at[sweep, 0], y_recv.at[sweep, 0], (x, y_down, z)),
            send(partial.at[sweep, 2], carry_in.at[sweep, 1], y_send.at[sweep, 1], y_recv.at[sweep, 1], (x, y_up, z)),
        ]
        for step in (0, 2, 1):
            z_copies[step].start()
        for step, copy in ((0, y_copies[0]), (2, y_copies[1])):
            z_copies[step].wait_recv()
            partial[sweep, step] = partial[sweep, step] + depth_in[sweep, step]
            copy.start()
        z_copies[1].wait_recv()
        for copy in y_copies:
            copy.wait_recv()
        for block in range(nblocks):
            for k in range(3):
                lanes = pl.ds(k * BLOCK, BLOCK)
                total = (
                    partial[sweep, 1, block, :, lanes]
                    + depth_in[sweep, 1, block, :, lanes]
                    + (carry_in[sweep, 0, block, :, lanes] + carry_in[sweep, 1, block, :, lanes])
                )
                out_ref[block, :, lanes] = respond(
                    field_ref[block, :, lanes] + coupling * total, block
                )

        @pl.when(sweep < ITERS - 1)
        def _():
            sources[sweep + 1, 1] = out_ref[...]
            for copy in x_copies(sweep + 1):
                copy.start()

        for copy in z_copies:
            copy.wait_send()
        for copy in y_copies:
            copy.wait_send()
        return carried

    lax.fori_loop(0, ITERS, sweep_step, 0)


def shards(positions, polarizability, applied_field, pair_codes, pair_counts):
    freqs = polarizability.shape[0]
    nblocks = positions.shape[1] // BLOCK
    pairs = pair_codes.shape[0]
    rows = 2 * freqs
    sizes = (lax.axis_size("gx"), lax.axis_size("gy"), nblocks, pairs)
    pos = positions.reshape(3, nblocks, BLOCK).transpose(1, 0, 2)
    pos = jnp.pad(pos, ((0, 0), (0, 5), (0, 0)))
    alpha = polarizability.reshape(freqs, 2, nblocks, BLOCK).transpose(2, 1, 0, 3)
    a1 = jnp.concatenate([alpha[:, 0], alpha[:, 0]], axis=1)
    a2 = jnp.concatenate([-alpha[:, 1], alpha[:, 1]], axis=1)
    field = applied_field.reshape(freqs, 2, 3, nblocks, BLOCK).transpose(3, 1, 0, 2, 4)
    field = field.reshape(nblocks, rows, 3 * BLOCK)
    vmem = pl.BlockSpec(memory_space=pltpu.VMEM)
    smem = pl.BlockSpec(memory_space=pltpu.SMEM)
    wide = 3 * BLOCK
    dma = pltpu.SemaphoreType.DMA
    out = pl.pallas_call(
        functools.partial(kernel, sizes),
        out_shape=jax.ShapeDtypeStruct((nblocks, rows, wide), jnp.float32),
        in_specs=[smem, smem, vmem, vmem, vmem, vmem],
        out_specs=vmem,
        scratch_shapes=[
            pltpu.VMEM((3, nblocks, 8, BLOCK), jnp.float32),
            pltpu.VMEM((6, nblocks, 8, BLOCK), jnp.float32),
            pltpu.VMEM((pairs, 2 * wide, wide), jnp.bfloat16),
            pltpu.VMEM((pairs * rows, 6 * nblocks * rows), jnp.float32),
            pltpu.VMEM((6 * nblocks * rows, pairs * rows), jnp.bfloat16),
            pltpu.VMEM((ITERS, 3, nblocks, rows, wide), jnp.float32),
            pltpu.VMEM((3, nblocks, 2 * rows, wide), jnp.bfloat16),
            pltpu.VMEM((pairs * rows, wide), jnp.float32),
            pltpu.VMEM((ITERS, 6, nblocks, rows, wide), jnp.float32),
            pltpu.VMEM((ITERS, 3, nblocks, rows, wide), jnp.float32),
            pltpu.VMEM((ITERS, 2, nblocks, rows, wide), jnp.float32),
            dma((7,)),
            dma((7,)),
            dma((ITERS, 2)),
            dma((ITERS, 2)),
            dma((ITERS, 3)),
            dma((ITERS, 3)),
            dma((ITERS, 2)),
            dma((ITERS, 2)),
        ],
        compiler_params=pltpu.CompilerParams(
            collective_id=0, has_side_effects=True, vmem_limit_bytes=40 * 1024 * 1024
        ),
    )(pair_codes, pair_counts, pos, a1, a2, field)
    out = out.reshape(nblocks, 2, freqs, 3, BLOCK).transpose(2, 1, 3, 0, 4)
    return out.reshape(freqs, 2, 3, nblocks * BLOCK)


def solution(mesh):
    in_specs = (
        P(None, ("gx", "gy", "gz")),
        P(None, None, ("gx", "gy", "gz")),
        P(None, None, None, ("gx", "gy", "gz")),
        P(("gx", "gy", "gz")),
        P(("gx", "gy", "gz")),
    )
    out_specs = P(None, None, None, ("gx", "gy", "gz"))
    return jax.shard_map(shards, mesh=mesh, in_specs=in_specs, out_specs=out_specs, check_vma=False)
```

```python
import functools
import math

import jax
import jax.numpy as jnp
from jax import lax
from jax.experimental import pallas as pl
from jax.experimental.pallas import tpu as pltpu
from jax.sharding import PartitionSpec as P

BLOCK = 128
ITERS = 4
UNROLL = 8

cell_width = 4.0
soften = 1.0
screen = 0.5
coupling = 0.8

CENTER = 0.54
SERIES = (
    0.806488610702616,
    0.7241185361715909,
    0.27511941992319955,
    -0.26086845400919295,
    0.2296813716405795,
    -0.17763507721765817,
    0.1043247007059023,
    -0.02452746718798479,
    -0.07547989643924369,
    0.2975431845822381,
    -0.5276853186117066,
    0.345520543574722,
)
MESH = pl.DeviceIdType.MESH


def split(value):
    high = value.astype(jnp.bfloat16)
    low = (value - high.astype(jnp.float32)).astype(jnp.bfloat16)
    return high, low


def kernel(
    sizes,
    codes_ref,
    count_ref,
    pos_ref,
    a1_ref,
    a2_ref,
    field_ref,
    out_ref,
    src_pos,
    tgt_pos,
    tensors,
    choose,
    chosen,
    sources,
    halves,
    contribs,
    partial,
    depth_in,
    carry_in,
    pos_send,
    pos_recv,
    x_send,
    x_recv,
    z_send,
    z_recv,
    y_send,
    y_recv,
):
    n_x, n_y, nblocks, pairs = sizes
    square = nblocks * nblocks
    rows = field_ref.shape[2]
    x = lax.axis_index("gx")
    y = lax.axis_index("gy")
    z = lax.axis_index("gz")
    x_up, x_down = lax.rem(x + 1, n_x), lax.rem(x + n_x - 1, n_x)
    y_up, y_down = lax.rem(y + 1, n_y), lax.rem(y + n_y - 1, n_y)
    other = 1 - z

    barrier = pltpu.get_barrier_semaphore()
    partners = (
        (x_up, y, z),
        (x_down, y, z),
        (x, y_up, z),
        (x, y_down, z),
        (x, y_up, other),
        (x, y_down, other),
        (x, y, other),
    )
    for partner in partners:
        pl.semaphore_signal(barrier, inc=1, device_id=partner, device_id_type=MESH)

    def respond(field, block):
        turned = jnp.concatenate([field[rows // 2 :], field[: rows // 2]], axis=0)
        return a1_ref[block] * field + a2_ref[block] * turned

    for k in range(3):
        for block in range(nblocks):
            sources[0, 1, k, block] = respond(field_ref[k, block], block)
    src_pos[1] = pos_ref[...]
    tgt_pos[1] = pos_ref[...]

    def send(src, dst, send_sem, recv_sem, device):
        return pltpu.make_async_remote_copy(
            src_ref=src,
            dst_ref=dst,
            send_sem=send_sem,
            recv_sem=recv_sem,
            device_id=device,
            device_id_type=MESH,
        )

    pl.semaphore_wait(barrier, len(partners))

    def x_copies(sweep, k):
        own = sources.at[sweep, 1, k]
        return (
            send(own, sources.at[sweep, 0, k], x_send.at[sweep, k, 0], x_recv.at[sweep, k, 0], (x_up, y, z)),
            send(own, sources.at[sweep, 2, k], x_send.at[sweep, k, 1], x_recv.at[sweep, k, 1], (x_down, y, z)),
        )

    pos_copies = (
        send(pos_ref, src_pos.at[0], pos_send.at[0], pos_recv.at[0], (x_up, y, z)),
        send(pos_ref, src_pos.at[2], pos_send.at[1], pos_recv.at[1], (x_down, y, z)),
        send(pos_ref, tgt_pos.at[0], pos_send.at[2], pos_recv.at[2], (x, y_up, z)),
        send(pos_ref, tgt_pos.at[2], pos_send.at[3], pos_recv.at[3], (x, y_down, z)),
        send(pos_ref, tgt_pos.at[3], pos_send.at[4], pos_recv.at[4], (x, y_up, other)),
        send(pos_ref, tgt_pos.at[5], pos_send.at[5], pos_recv.at[5], (x, y_down, other)),
        send(pos_ref, tgt_pos.at[4], pos_send.at[6], pos_recv.at[6], (x, y, other)),
    )
    for copy in pos_copies:
        copy.start()
    for k in range(3):
        for copy in x_copies(0, k):
            copy.start()
    for copy in pos_copies:
        copy.wait()

    def decode(entry):
        code = codes_ref[entry]
        src_block = code % nblocks
        tgt_block = code // nblocks % nblocks
        depth_tgt = code // square % 2
        step_y = code // (2 * square) % 3
        step_x = code // (6 * square)
        turned_depth = (depth_tgt + z) % 2
        return src_block, tgt_block, turned_depth, step_y, step_x

    def build(entry, carried):
        src_block, tgt_block, depth, step_y, step_x = decode(entry)
        src = src_pos[step_x, src_block].T
        tgt = tgt_pos[depth * 3 + step_y, tgt_block]
        shift_x = (step_x - 1).astype(jnp.float32) * -cell_width
        shift_y = (step_y - 1).astype(jnp.float32) * cell_width
        disp = [
            tgt[0:1] - src[:, 0:1] + shift_x,
            tgt[1:2] - src[:, 1:2] + shift_y,
            tgt[2:3] - src[:, 2:3],
        ]
        dist_sq = disp[0] * disp[0] + disp[1] * disp[1] + disp[2] * disp[2] + soften * soften
        inv = lax.rsqrt(dist_sq)
        inv_sq = inv * inv
        offset = inv - CENTER
        series = jnp.full_like(offset, SERIES[-1])
        for term in SERIES[-2::-1]:
            series = series * offset + term
        scale = jnp.exp(-screen * screen * dist_sq) * inv_sq
        b_term = scale * series
        c_term = scale * (3.0 * inv_sq * series + 2.0 * screen * screen / math.sqrt(math.pi))
        for a in range(3):
            scaled = c_term * disp[a]
            for b in range(a, 3):
                value = scaled * disp[b]
                if a == b:
                    value = value - b_term
                high, low = split(value)
                for r, c in {(a, b), (b, a)}:
                    lanes = pl.ds(c * BLOCK, BLOCK)
                    tensors[entry, r, pl.ds(0, BLOCK), lanes] = high
                    tensors[entry, r, pl.ds(BLOCK, BLOCK), lanes] = low
        slot = (depth * 3 + step_y) * nblocks + tgt_block
        slot = jnp.where(entry < count_ref[0], slot, -1)
        shape = (rows, 6 * nblocks * rows)
        column = lax.broadcasted_iota(jnp.int32, shape, 1)
        row = lax.broadcasted_iota(jnp.int32, shape, 0)
        choose[pl.ds(entry * rows, rows), :] = jnp.where(column == slot * rows + row, 1.0, 0.0)
        return carried

    lax.fori_loop(0, pairs, build, 0)
    chosen[...] = choose[...].T.astype(jnp.bfloat16)

    def sweep_step(sweep, carried):
        for k in range(3):
            for copy in x_copies(sweep, k):
                copy.wait()
            for step in range(3):
                for block in range(nblocks):
                    high, low = split(sources[sweep, step, k, block])
                    halves[k, step, block] = jnp.concatenate([high, low], axis=0)

            def pair_step(group, carried):
                for member in range(UNROLL):
                    entry = group * UNROLL + member
                    src_block, _, _, _, step_x = decode(entry)
                    both = halves[k, step_x, src_block]
                    both = jnp.concatenate([both, both], axis=1)
                    result = jnp.dot(both, tensors[entry, k], preferred_element_type=jnp.float32)
                    result = result[:rows] + result[rows:]
                    place = pl.ds(entry * rows, rows)
                    contribs[place, :] = result if k == 0 else contribs[place, :] + result
                return carried

            lax.fori_loop(0, pairs // UNROLL, pair_step, 0)

        z_copies = [
            send(
                partial.at[sweep, k, pl.ds(3, 3)],
                depth_in.at[sweep, k],
                z_send.at[sweep, k],
                z_recv.at[sweep, k],
                (x, y, other),
            )
            for k in range(3)
        ]
        y_copies = [
            (
                send(
                    partial.at[sweep, k, 0],
                    carry_in.at[sweep, k, 0],
                    y_send.at[sweep, k, 0],
                    y_recv.at[sweep, k, 0],
                    (x, y_down, z),
                ),
                send(
                    partial.at[sweep, k, 2],
                    carry_in.at[sweep, k, 1],
                    y_send.at[sweep, k, 1],
                    y_recv.at[sweep, k, 1],
                    (x, y_up, z),
                ),
            )
            for k in range(3)
        ]
        for k in range(3):
            high, low = split(contribs[:, pl.ds(k * BLOCK, BLOCK)])
            both = jnp.concatenate([high, low], axis=1)
            merged = jnp.dot(chosen[...], both, preferred_element_type=jnp.float32)
            merged = merged[:, :BLOCK] + merged[:, BLOCK:]
            partial[sweep, k] = merged.reshape(6, nblocks, rows, BLOCK)
            z_copies[k].start()
        for k in range(3):
            z_copies[k].wait_recv()
            for step, copy in zip((0, 2), y_copies[k]):
                partial[sweep, k, step] = partial[sweep, k, step] + depth_in[sweep, k, step]
                copy.start()
        for k in range(3):
            for copy in y_copies[k]:
                copy.wait_recv()
            for block in range(nblocks):
                total = (
                    partial[sweep, k, 1, block]
                    + depth_in[sweep, k, 1, block]
                    + (carry_in[sweep, k, 0, block] + carry_in[sweep, k, 1, block])
                )
                out_ref[k, block] = respond(field_ref[k, block] + coupling * total, block)

            @pl.when(sweep < ITERS - 1)
            def _():
                sources[sweep + 1, 1, k] = out_ref[k]
                for copy in x_copies(sweep + 1, k):
                    copy.start()

        for k in range(3):
            z_copies[k].wait_send()
            for copy in y_copies[k]:
                copy.wait_send()
        return carried

    lax.fori_loop(0, ITERS, sweep_step, 0)


def shards(positions, polarizability, applied_field, pair_codes, pair_counts):
    freqs = polarizability.shape[0]
    nblocks = positions.shape[1] // BLOCK
    pairs = pair_codes.shape[0]
    rows = 2 * freqs
    sizes = (lax.axis_size("gx"), lax.axis_size("gy"), nblocks, pairs)
    pos = positions.reshape(3, nblocks, BLOCK).transpose(1, 0, 2)
    pos = jnp.pad(pos, ((0, 0), (0, 5), (0, 0)))
    alpha = polarizability.reshape(freqs, 2, nblocks, BLOCK).transpose(2, 1, 0, 3)
    a1 = jnp.concatenate([alpha[:, 0], alpha[:, 0]], axis=1)
    a2 = jnp.concatenate([-alpha[:, 1], alpha[:, 1]], axis=1)
    field = applied_field.reshape(freqs, 2, 3, nblocks, BLOCK).transpose(2, 3, 1, 0, 4)
    field = field.reshape(3, nblocks, rows, BLOCK)
    vmem = pl.BlockSpec(memory_space=pltpu.VMEM)
    smem = pl.BlockSpec(memory_space=pltpu.SMEM)
    wide = 3 * BLOCK
    dma = pltpu.SemaphoreType.DMA
    out = pl.pallas_call(
        functools.partial(kernel, sizes),
        out_shape=jax.ShapeDtypeStruct((3, nblocks, rows, BLOCK), jnp.float32),
        in_specs=[smem, smem, vmem, vmem, vmem, vmem],
        out_specs=vmem,
        scratch_shapes=[
            pltpu.VMEM((3, nblocks, 8, BLOCK), jnp.float32),
            pltpu.VMEM((6, nblocks, 8, BLOCK), jnp.float32),
            pltpu.VMEM((pairs, 3, 2 * BLOCK, wide), jnp.bfloat16),
            pltpu.VMEM((pairs * rows, 6 * nblocks * rows), jnp.float32),
            pltpu.VMEM((6 * nblocks * rows, pairs * rows), jnp.bfloat16),
            pltpu.VMEM((ITERS, 3, 3, nblocks, rows, BLOCK), jnp.float32),
            pltpu.VMEM((3, 3, nblocks, 2 * rows, BLOCK), jnp.bfloat16),
            pltpu.VMEM((pairs * rows, wide), jnp.float32),
            pltpu.VMEM((ITERS, 3, 6, nblocks, rows, BLOCK), jnp.float32),
            pltpu.VMEM((ITERS, 3, 3, nblocks, rows, BLOCK), jnp.float32),
            pltpu.VMEM((ITERS, 3, 2, nblocks, rows, BLOCK), jnp.float32),
            dma((7,)),
            dma((7,)),
            dma((ITERS, 3, 2)),
            dma((ITERS, 3, 2)),
            dma((ITERS, 3)),
            dma((ITERS, 3)),
            dma((ITERS, 3, 2)),
            dma((ITERS, 3, 2)),
        ],
        compiler_params=pltpu.CompilerParams(
            collective_id=0, has_side_effects=True, vmem_limit_bytes=40 * 1024 * 1024
        ),
    )(pair_codes, pair_counts, pos, a1, a2, field)
    out = out.reshape(3, nblocks, 2, freqs, BLOCK).transpose(3, 2, 0, 1, 4)
    return out.reshape(freqs, 2, 3, nblocks * BLOCK)


def solution(mesh):
    in_specs = (
        P(None, ("gx", "gy", "gz")),
        P(None, None, ("gx", "gy", "gz")),
        P(None, None, None, ("gx", "gy", "gz")),
        P(("gx", "gy", "gz")),
        P(("gx", "gy", "gz")),
    )
    out_specs = P(None, None, None, ("gx", "gy", "gz"))
    return jax.shard_map(shards, mesh=mesh, in_specs=in_specs, out_specs=out_specs, check_vma=False)
```

```python
import functools
import math

import jax
import jax.numpy as jnp
from jax import lax
from jax.experimental import pallas as pl
from jax.experimental.pallas import tpu as pltpu
from jax.sharding import PartitionSpec as P

BLOCK = 128
ITERS = 4
UNROLL = 8

cell_width = 4.0
soften = 1.0
screen = 0.5
coupling = 0.8

CENTER = 0.54
SERIES = (
    0.806488610702616,
    0.7241185361715909,
    0.27511941992319955,
    -0.26086845400919295,
    0.2296813716405795,
    -0.17763507721765817,
    0.1043247007059023,
    -0.02452746718798479,
    -0.07547989643924369,
    0.2975431845822381,
    -0.5276853186117066,
    0.345520543574722,
)
MESH = pl.DeviceIdType.MESH


def split(value):
    high = value.astype(jnp.bfloat16)
    low = (value - high.astype(jnp.float32)).astype(jnp.bfloat16)
    return high, low


def kernel(
    sizes,
    codes_ref,
    count_ref,
    pos_ref,
    a1_ref,
    a2_ref,
    field_ref,
    out_ref,
    src_pos,
    tgt_pos,
    tensors,
    choose,
    chosen,
    sources,
    halves,
    contribs,
    partial,
    depth_in,
    carry_in,
    pos_send,
    pos_recv,
    x_send,
    x_recv,
    z_send,
    z_recv,
    y_send,
    y_recv,
):
    n_x, n_y, nblocks, pairs = sizes
    square = nblocks * nblocks
    rows = field_ref.shape[2]
    x = lax.axis_index("gx")
    y = lax.axis_index("gy")
    z = lax.axis_index("gz")
    x_up, x_down = lax.rem(x + 1, n_x), lax.rem(x + n_x - 1, n_x)
    y_up, y_down = lax.rem(y + 1, n_y), lax.rem(y + n_y - 1, n_y)
    other = 1 - z

    barrier = pltpu.get_barrier_semaphore()
    partners = (
        (x_up, y, z),
        (x_down, y, z),
        (x, y_up, z),
        (x, y_down, z),
        (x, y_up, other),
        (x, y_down, other),
        (x, y, other),
    )
    for partner in partners:
        pl.semaphore_signal(barrier, inc=1, device_id=partner, device_id_type=MESH)

    def respond(field, block):
        turned = jnp.concatenate([field[rows // 2 :], field[: rows // 2]], axis=0)
        return a1_ref[block] * field + a2_ref[block] * turned

    for k in range(3):
        for block in range(nblocks):
            sources[0, 1, k, block] = respond(field_ref[k, block], block)
    src_pos[1] = pos_ref[...]
    tgt_pos[1] = pos_ref[...]

    def send(src, dst, send_sem, recv_sem, device):
        return pltpu.make_async_remote_copy(
            src_ref=src,
            dst_ref=dst,
            send_sem=send_sem,
            recv_sem=recv_sem,
            device_id=device,
            device_id_type=MESH,
        )

    pl.semaphore_wait(barrier, len(partners))

    def x_copies(sweep, k):
        own = sources.at[sweep, 1, k]
        return (
            send(own, sources.at[sweep, 0, k], x_send.at[sweep, k, 0], x_recv.at[sweep, k, 0], (x_up, y, z)),
            send(own, sources.at[sweep, 2, k], x_send.at[sweep, k, 1], x_recv.at[sweep, k, 1], (x_down, y, z)),
        )

    pos_copies = (
        send(pos_ref, src_pos.at[0], pos_send.at[0], pos_recv.at[0], (x_up, y, z)),
        send(pos_ref, src_pos.at[2], pos_send.at[1], pos_recv.at[1], (x_down, y, z)),
        send(pos_ref, tgt_pos.at[0], pos_send.at[2], pos_recv.at[2], (x, y_up, z)),
        send(pos_ref, tgt_pos.at[2], pos_send.at[3], pos_recv.at[3], (x, y_down, z)),
        send(pos_ref, tgt_pos.at[3], pos_send.at[4], pos_recv.at[4], (x, y_up, other)),
        send(pos_ref, tgt_pos.at[5], pos_send.at[5], pos_recv.at[5], (x, y_down, other)),
        send(pos_ref, tgt_pos.at[4], pos_send.at[6], pos_recv.at[6], (x, y, other)),
    )
    for copy in pos_copies:
        copy.start()
    for k in range(3):
        for copy in x_copies(0, k):
            copy.start()
    for copy in pos_copies:
        copy.wait()

    def decode(entry):
        code = codes_ref[entry]
        src_block = code % nblocks
        tgt_block = code // nblocks % nblocks
        depth_tgt = code // square % 2
        step_y = code // (2 * square) % 3
        step_x = code // (6 * square)
        turned_depth = (depth_tgt + z) % 2
        return src_block, tgt_block, turned_depth, step_y, step_x

    def build(entry, carried):
        src_block, tgt_block, depth, step_y, step_x = decode(entry)
        src = src_pos[step_x, src_block].T
        tgt = tgt_pos[depth * 3 + step_y, tgt_block]
        shift_x = (step_x - 1).astype(jnp.float32) * -cell_width
        shift_y = (step_y - 1).astype(jnp.float32) * cell_width
        disp = [
            tgt[0:1] - src[:, 0:1] + shift_x,
            tgt[1:2] - src[:, 1:2] + shift_y,
            tgt[2:3] - src[:, 2:3],
        ]
        dist_sq = disp[0] * disp[0] + disp[1] * disp[1] + disp[2] * disp[2] + soften * soften
        inv = lax.rsqrt(dist_sq)
        inv_sq = inv * inv
        offset = inv - CENTER
        series = jnp.full_like(offset, SERIES[-1])
        for term in SERIES[-2::-1]:
            series = series * offset + term
        scale = jnp.exp(-screen * screen * dist_sq) * inv_sq
        b_term = scale * series
        c_term = scale * (3.0 * inv_sq * series + 2.0 * screen * screen / math.sqrt(math.pi))
        for t in range(3):
            scaled = c_term * disp[t]
            pieces = (scaled * disp[t] - b_term, scaled * disp[(t + 1) % 3])
            for part, value in enumerate(pieces):
                high, low = split(value)
                lanes = pl.ds(part * BLOCK, BLOCK)
                tensors[entry, t, pl.ds(0, BLOCK), lanes] = high
                tensors[entry, t, pl.ds(BLOCK, BLOCK), lanes] = low
        slot = (depth * 3 + step_y) * nblocks + tgt_block
        slot = jnp.where(entry < count_ref[0], slot, -1)
        shape = (rows, 6 * nblocks * rows)
        column = lax.broadcasted_iota(jnp.int32, shape, 1)
        row = lax.broadcasted_iota(jnp.int32, shape, 0)
        choose[pl.ds(entry * rows, rows), :] = jnp.where(column == slot * rows + row, 1.0, 0.0)
        return carried

    lax.fori_loop(0, pairs, build, 0)
    chosen[...] = choose[...].T.astype(jnp.bfloat16)

    def sweep_step(sweep, carried):
        def arrive(k):
            for copy in x_copies(sweep, k):
                copy.wait()
            for step in range(3):
                for block in range(nblocks):
                    high, low = split(sources[sweep, step, k, block])
                    both = jnp.concatenate([high, low], axis=0)
                    halves[step, block, pl.ds(k * 2 * rows, 2 * rows)] = both

        def tile_dot(entry, t, step_x, src_block):
            if t < 2:
                both = halves[step_x, src_block, pl.ds(t * 2 * rows, 4 * rows)]
            else:
                both = jnp.concatenate(
                    [
                        halves[step_x, src_block, pl.ds(4 * rows, 2 * rows)],
                        halves[step_x, src_block, pl.ds(0, 2 * rows)],
                    ],
                    axis=0,
                )
            both = jnp.concatenate([both, both], axis=1)
            result = jnp.dot(both, tensors[entry, t], preferred_element_type=jnp.float32)
            first = result[:rows] + result[rows : 2 * rows]
            second = result[2 * rows : 3 * rows, BLOCK:] + result[3 * rows :, BLOCK:]
            return first[:, :BLOCK] + second, first[:, BLOCK:]

        def early_step(group, carried):
            for member in range(UNROLL):
                entry = group * UNROLL + member
                src_block, _, _, _, step_x = decode(entry)
                to_x, to_y = tile_dot(entry, 0, step_x, src_block)
                place = pl.ds(entry * rows, rows)
                contribs[place, pl.ds(0, BLOCK)] = to_x
                contribs[place, pl.ds(BLOCK, BLOCK)] = to_y
            return carried

        def late_step(group, carried):
            for member in range(UNROLL):
                entry = group * UNROLL + member
                src_block, _, _, _, step_x = decode(entry)
                to_y, from_y = tile_dot(entry, 1, step_x, src_block)
                to_z, to_x = tile_dot(entry, 2, step_x, src_block)
                place = pl.ds(entry * rows, rows)
                lanes = [pl.ds(k * BLOCK, BLOCK) for k in range(3)]
                contribs[place, lanes[0]] = contribs[place, lanes[0]] + to_x
                contribs[place, lanes[1]] = contribs[place, lanes[1]] + to_y
                contribs[place, lanes[2]] = from_y + to_z
            return carried

        arrive(0)
        arrive(1)
        lax.fori_loop(0, pairs // UNROLL, early_step, 0)
        arrive(2)
        lax.fori_loop(0, pairs // UNROLL, late_step, 0)

        z_copies = [
            send(
                partial.at[sweep, k, pl.ds(3, 3)],
                depth_in.at[sweep, k],
                z_send.at[sweep, k],
                z_recv.at[sweep, k],
                (x, y, other),
            )
            for k in range(3)
        ]
        y_copies = [
            (
                send(
                    partial.at[sweep, k, 0],
                    carry_in.at[sweep, k, 0],
                    y_send.at[sweep, k, 0],
                    y_recv.at[sweep, k, 0],
                    (x, y_down, z),
                ),
                send(
                    partial.at[sweep, k, 2],
                    carry_in.at[sweep, k, 1],
                    y_send.at[sweep, k, 1],
                    y_recv.at[sweep, k, 1],
                    (x, y_up, z),
                ),
            )
            for k in range(3)
        ]
        for k in range(3):
            high, low = split(contribs[:, pl.ds(k * BLOCK, BLOCK)])
            both = jnp.concatenate([high, low], axis=1)
            merged = jnp.dot(chosen[...], both, preferred_element_type=jnp.float32)
            merged = merged[:, :BLOCK] + merged[:, BLOCK:]
            partial[sweep, k] = merged.reshape(6, nblocks, rows, BLOCK)
            z_copies[k].start()
        for k in range(3):
            z_copies[k].wait_recv()
            for step, copy in zip((0, 2), y_copies[k]):
                partial[sweep, k, step] = partial[sweep, k, step] + depth_in[sweep, k, step]
                copy.start()
        for k in range(3):
            for copy in y_copies[k]:
                copy.wait_recv()
            for block in range(nblocks):
                total = (
                    partial[sweep, k, 1, block]
                    + depth_in[sweep, k, 1, block]
                    + (carry_in[sweep, k, 0, block] + carry_in[sweep, k, 1, block])
                )
                out_ref[k, block] = respond(field_ref[k, block] + coupling * total, block)

            @pl.when(sweep < ITERS - 1)
            def _():
                sources[sweep + 1, 1, k] = out_ref[k]
                for copy in x_copies(sweep + 1, k):
                    copy.start()

        for k in range(3):
            z_copies[k].wait_send()
            for copy in y_copies[k]:
                copy.wait_send()
        return carried

    lax.fori_loop(0, ITERS, sweep_step, 0)


def shards(positions, polarizability, applied_field, pair_codes, pair_counts):
    freqs = polarizability.shape[0]
    nblocks = positions.shape[1] // BLOCK
    pairs = pair_codes.shape[0]
    rows = 2 * freqs
    sizes = (lax.axis_size("gx"), lax.axis_size("gy"), nblocks, pairs)
    pos = positions.reshape(3, nblocks, BLOCK).transpose(1, 0, 2)
    pos = jnp.pad(pos, ((0, 0), (0, 5), (0, 0)))
    alpha = polarizability.reshape(freqs, 2, nblocks, BLOCK).transpose(2, 1, 0, 3)
    a1 = jnp.concatenate([alpha[:, 0], alpha[:, 0]], axis=1)
    a2 = jnp.concatenate([-alpha[:, 1], alpha[:, 1]], axis=1)
    field = applied_field.reshape(freqs, 2, 3, nblocks, BLOCK).transpose(2, 3, 1, 0, 4)
    field = field.reshape(3, nblocks, rows, BLOCK)
    vmem = pl.BlockSpec(memory_space=pltpu.VMEM)
    smem = pl.BlockSpec(memory_space=pltpu.SMEM)
    wide = 3 * BLOCK
    dma = pltpu.SemaphoreType.DMA
    out = pl.pallas_call(
        functools.partial(kernel, sizes),
        out_shape=jax.ShapeDtypeStruct((3, nblocks, rows, BLOCK), jnp.float32),
        in_specs=[smem, smem, vmem, vmem, vmem, vmem],
        out_specs=vmem,
        scratch_shapes=[
            pltpu.VMEM((3, nblocks, 8, BLOCK), jnp.float32),
            pltpu.VMEM((6, nblocks, 8, BLOCK), jnp.float32),
            pltpu.VMEM((pairs, 3, 2 * BLOCK, 2 * BLOCK), jnp.bfloat16),
            pltpu.VMEM((pairs * rows, 6 * nblocks * rows), jnp.float32),
            pltpu.VMEM((6 * nblocks * rows, pairs * rows), jnp.bfloat16),
            pltpu.VMEM((ITERS, 3, 3, nblocks, rows, BLOCK), jnp.float32),
            pltpu.VMEM((3, nblocks, 6 * rows, BLOCK), jnp.bfloat16),
            pltpu.VMEM((pairs * rows, wide), jnp.float32),
            pltpu.VMEM((ITERS, 3, 6, nblocks, rows, BLOCK), jnp.float32),
            pltpu.VMEM((ITERS, 3, 3, nblocks, rows, BLOCK), jnp.float32),
            pltpu.VMEM((ITERS, 3, 2, nblocks, rows, BLOCK), jnp.float32),
            dma((7,)),
            dma((7,)),
            dma((ITERS, 3, 2)),
            dma((ITERS, 3, 2)),
            dma((ITERS, 3)),
            dma((ITERS, 3)),
            dma((ITERS, 3, 2)),
            dma((ITERS, 3, 2)),
        ],
        compiler_params=pltpu.CompilerParams(
            collective_id=0, has_side_effects=True, vmem_limit_bytes=40 * 1024 * 1024
        ),
    )(pair_codes, pair_counts, pos, a1, a2, field)
    out = out.reshape(3, nblocks, 2, freqs, BLOCK).transpose(3, 2, 0, 1, 4)
    return out.reshape(freqs, 2, 3, nblocks * BLOCK)


def solution(mesh):
    in_specs = (
        P(None, ("gx", "gy", "gz")),
        P(None, None, ("gx", "gy", "gz")),
        P(None, None, None, ("gx", "gy", "gz")),
        P(("gx", "gy", "gz")),
        P(("gx", "gy", "gz")),
    )
    out_specs = P(None, None, None, ("gx", "gy", "gz"))
    return jax.shard_map(shards, mesh=mesh, in_specs=in_specs, out_specs=out_specs, check_vma=False)
```

```python
import functools
import math

import jax
import jax.numpy as jnp
from jax import lax
from jax.experimental import pallas as pl
from jax.experimental.pallas import tpu as pltpu
from jax.sharding import PartitionSpec as P

BLOCK = 128
ITERS = 4
UNROLL = 8
STRIP = 64

cell_width = 4.0
soften = 1.0
screen = 0.5
coupling = 0.8

CENTER = 0.54
SERIES = (
    0.806488610702616,
    0.7241185361715909,
    0.27511941992319955,
    -0.26086845400919295,
    0.2296813716405795,
    -0.17763507721765817,
    0.1043247007059023,
    -0.02452746718798479,
    -0.07547989643924369,
    0.2975431845822381,
    -0.5276853186117066,
    0.345520543574722,
)
MESH = pl.DeviceIdType.MESH


def split(value):
    high = value.astype(jnp.bfloat16)
    low = (value - high.astype(jnp.float32)).astype(jnp.bfloat16)
    return high, low


def kernel(
    sizes,
    codes_ref,
    count_ref,
    raw_pos,
    raw_alpha,
    raw_field,
    out_ref,
    a1_ref,
    a2_ref,
    field_ref,
    src_pos,
    tgt_pos,
    tensors,
    choose,
    chosen,
    sources,
    halves,
    contribs,
    latest,
    partial,
    depth_in,
    carry_in,
    pos_send,
    pos_recv,
    x_send,
    x_recv,
    z_send,
    z_recv,
    y_send,
    y_recv,
):
    n_x, n_y, nblocks, pairs = sizes
    square = nblocks * nblocks
    rows = field_ref.shape[2]
    x = lax.axis_index("gx")
    y = lax.axis_index("gy")
    z = lax.axis_index("gz")
    x_up, x_down = lax.rem(x + 1, n_x), lax.rem(x + n_x - 1, n_x)
    y_up, y_down = lax.rem(y + 1, n_y), lax.rem(y + n_y - 1, n_y)
    other = 1 - z

    barrier = pltpu.get_barrier_semaphore()
    partners = (
        (x_up, y, z),
        (x_down, y, z),
        (x, y_up, z),
        (x, y_down, z),
        (x, y_up, other),
        (x, y_down, other),
        (x, y, other),
    )
    for partner in partners:
        pl.semaphore_signal(barrier, inc=1, device_id=partner, device_id_type=MESH)

    def respond(field, block):
        turned = jnp.concatenate([field[rows // 2 :], field[: rows // 2]], axis=0)
        return a1_ref[block] * field + a2_ref[block] * turned

    src_pos[1] = jnp.zeros_like(src_pos[1])
    for block in range(nblocks):
        span = pl.ds(block * BLOCK, BLOCK)
        src_pos[1, block, pl.ds(0, 3), :] = raw_pos[:, span]
        real, imag = raw_alpha[:, 0, span], raw_alpha[:, 1, span]
        a1_ref[block] = jnp.concatenate([real, real], axis=0)
        a2_ref[block] = jnp.concatenate([-imag, imag], axis=0)
        for k in range(3):
            field_ref[k, block] = jnp.concatenate(
                [raw_field[:, k, 0, span], raw_field[:, k, 1, span]], axis=0
            )
    tgt_pos[1] = src_pos[1]
    for k in range(3):
        for block in range(nblocks):
            sources[0, 1, k, block] = respond(field_ref[k, block], block)

    def send(src, dst, send_sem, recv_sem, device):
        return pltpu.make_async_remote_copy(
            src_ref=src,
            dst_ref=dst,
            send_sem=send_sem,
            recv_sem=recv_sem,
            device_id=device,
            device_id_type=MESH,
        )

    pl.semaphore_wait(barrier, len(partners))

    def x_copies(sweep, k):
        own = sources.at[sweep, 1, k]
        return (
            send(own, sources.at[sweep, 0, k], x_send.at[sweep, k, 0], x_recv.at[sweep, k, 0], (x_up, y, z)),
            send(own, sources.at[sweep, 2, k], x_send.at[sweep, k, 1], x_recv.at[sweep, k, 1], (x_down, y, z)),
        )

    pos_copies = (
        send(src_pos.at[1], src_pos.at[0], pos_send.at[0], pos_recv.at[0], (x_up, y, z)),
        send(src_pos.at[1], src_pos.at[2], pos_send.at[1], pos_recv.at[1], (x_down, y, z)),
        send(src_pos.at[1], tgt_pos.at[0], pos_send.at[2], pos_recv.at[2], (x, y_up, z)),
        send(src_pos.at[1], tgt_pos.at[2], pos_send.at[3], pos_recv.at[3], (x, y_down, z)),
        send(src_pos.at[1], tgt_pos.at[3], pos_send.at[4], pos_recv.at[4], (x, y_up, other)),
        send(src_pos.at[1], tgt_pos.at[5], pos_send.at[5], pos_recv.at[5], (x, y_down, other)),
        send(src_pos.at[1], tgt_pos.at[4], pos_send.at[6], pos_recv.at[6], (x, y, other)),
    )
    for copy in pos_copies:
        copy.start()
    for k in range(3):
        for copy in x_copies(0, k):
            copy.start()
    for copy in pos_copies:
        copy.wait()

    def decode(entry):
        code = codes_ref[entry]
        src_block = code % nblocks
        tgt_block = code // nblocks % nblocks
        depth_tgt = code // square % 2
        step_y = code // (2 * square) % 3
        step_x = code // (6 * square)
        turned_depth = (depth_tgt + z) % 2
        return src_block, tgt_block, turned_depth, step_y, step_x

    def build(entry, carried):
        src_block, tgt_block, depth, step_y, step_x = decode(entry)
        src = src_pos[step_x, src_block].T
        tgt = tgt_pos[depth * 3 + step_y, tgt_block]
        shift_x = (step_x - 1).astype(jnp.float32) * -cell_width
        shift_y = (step_y - 1).astype(jnp.float32) * cell_width
        for at in range(0, BLOCK, STRIP):
            strip = slice(at, at + STRIP)
            disp = [
                tgt[0:1] - src[strip, 0:1] + shift_x,
                tgt[1:2] - src[strip, 1:2] + shift_y,
                tgt[2:3] - src[strip, 2:3],
            ]
            dist_sq = disp[0] * disp[0] + disp[1] * disp[1] + disp[2] * disp[2] + soften * soften
            inv = lax.rsqrt(dist_sq)
            inv_sq = inv * inv
            offset = inv - CENTER
            series = jnp.full_like(offset, SERIES[-1])
            for term in SERIES[-2::-1]:
                series = series * offset + term
            scale = jnp.exp(-screen * screen * dist_sq) * inv_sq
            b_term = scale * series
            c_term = scale * (3.0 * inv_sq * series + 2.0 * screen * screen / math.sqrt(math.pi))
            for t in range(3):
                scaled = c_term * disp[t]
                pieces = (scaled * disp[t] - b_term, scaled * disp[(t + 1) % 3])
                for part, value in enumerate(pieces):
                    high, low = split(value)
                    lanes = pl.ds(part * BLOCK, BLOCK)
                    tensors[entry, t, pl.ds(at, STRIP), lanes] = high
                    tensors[entry, t, pl.ds(BLOCK + at, STRIP), lanes] = low
        slot = (depth * 3 + step_y) * nblocks + tgt_block
        slot = jnp.where(entry < count_ref[0], slot, -1)
        shape = (rows, 6 * nblocks * rows)
        column = lax.broadcasted_iota(jnp.int32, shape, 1)
        row = lax.broadcasted_iota(jnp.int32, shape, 0)
        choose[pl.ds(entry * rows, rows), :] = jnp.where(column == slot * rows + row, 1.0, 0.0)
        return carried

    def build_two(group, carried):
        return build(group * 2 + 1, build(group * 2, carried))

    lax.fori_loop(0, pairs // 2, build_two, 0)
    chosen[...] = choose[...].T.astype(jnp.bfloat16)

    def sweep_step(sweep, carried):
        def arrive(k):
            for copy in x_copies(sweep, k):
                copy.wait()
            for step in range(3):
                for block in range(nblocks):
                    high, low = split(sources[sweep, step, k, block])
                    both = jnp.concatenate([high, low], axis=0)
                    halves[step, block, pl.ds(k * 2 * rows, 2 * rows)] = both

        def tile_dot(entry, t, step_x, src_block):
            if t < 2:
                both = halves[step_x, src_block, pl.ds(t * 2 * rows, 4 * rows)]
            else:
                both = jnp.concatenate(
                    [
                        halves[step_x, src_block, pl.ds(4 * rows, 2 * rows)],
                        halves[step_x, src_block, pl.ds(0, 2 * rows)],
                    ],
                    axis=0,
                )
            both = jnp.concatenate([both, both], axis=1)
            result = jnp.dot(both, tensors[entry, t], preferred_element_type=jnp.float32)
            first = result[:rows] + result[rows : 2 * rows]
            second = result[2 * rows : 3 * rows, BLOCK:] + result[3 * rows :, BLOCK:]
            return first[:, :BLOCK] + second, first[:, BLOCK:]

        def early_step(group, carried):
            for member in range(UNROLL):
                entry = group * UNROLL + member
                src_block, _, _, _, step_x = decode(entry)
                to_x, to_y = tile_dot(entry, 0, step_x, src_block)
                place = pl.ds(entry * rows, rows)
                contribs[place, pl.ds(0, BLOCK)] = to_x
                contribs[place, pl.ds(BLOCK, BLOCK)] = to_y
            return carried

        def late_step(group, carried):
            for member in range(UNROLL):
                entry = group * UNROLL + member
                src_block, _, _, _, step_x = decode(entry)
                to_y, from_y = tile_dot(entry, 1, step_x, src_block)
                to_z, to_x = tile_dot(entry, 2, step_x, src_block)
                place = pl.ds(entry * rows, rows)
                lanes = [pl.ds(k * BLOCK, BLOCK) for k in range(3)]
                contribs[place, lanes[0]] = contribs[place, lanes[0]] + to_x
                contribs[place, lanes[1]] = contribs[place, lanes[1]] + to_y
                contribs[place, lanes[2]] = from_y + to_z
            return carried

        arrive(0)
        arrive(1)
        lax.fori_loop(0, pairs // UNROLL, early_step, 0)
        arrive(2)
        lax.fori_loop(0, pairs // UNROLL, late_step, 0)

        z_copies = [
            send(
                partial.at[sweep, k, pl.ds(3, 3)],
                depth_in.at[sweep, k],
                z_send.at[sweep, k],
                z_recv.at[sweep, k],
                (x, y, other),
            )
            for k in range(3)
        ]
        y_copies = [
            (
                send(
                    partial.at[sweep, k, 0],
                    carry_in.at[sweep, k, 0],
                    y_send.at[sweep, k, 0],
                    y_recv.at[sweep, k, 0],
                    (x, y_down, z),
                ),
                send(
                    partial.at[sweep, k, 2],
                    carry_in.at[sweep, k, 1],
                    y_send.at[sweep, k, 1],
                    y_recv.at[sweep, k, 1],
                    (x, y_up, z),
                ),
            )
            for k in range(3)
        ]
        for k in range(3):
            high, low = split(contribs[:, pl.ds(k * BLOCK, BLOCK)])
            both = jnp.concatenate([high, low], axis=1)
            merged = jnp.dot(chosen[...], both, preferred_element_type=jnp.float32)
            merged = merged[:, :BLOCK] + merged[:, BLOCK:]
            partial[sweep, k] = merged.reshape(6, nblocks, rows, BLOCK)
            z_copies[k].start()
        for k in range(3):
            z_copies[k].wait_recv()
            for step, copy in zip((0, 2), y_copies[k]):
                partial[sweep, k, step] = partial[sweep, k, step] + depth_in[sweep, k, step]
                copy.start()
        for k in range(3):
            for copy in y_copies[k]:
                copy.wait_recv()
            for block in range(nblocks):
                total = (
                    partial[sweep, k, 1, block]
                    + depth_in[sweep, k, 1, block]
                    + (carry_in[sweep, k, 0, block] + carry_in[sweep, k, 1, block])
                )
                dipole = respond(field_ref[k, block] + coupling * total, block)
                latest[k, block] = dipole

            @pl.when(sweep < ITERS - 1)
            def _():
                sources[sweep + 1, 1, k] = latest[k]
                for copy in x_copies(sweep + 1, k):
                    copy.start()

        for k in range(3):
            z_copies[k].wait_send()
            for copy in y_copies[k]:
                copy.wait_send()
        return carried

    lax.fori_loop(0, ITERS, sweep_step, 0)
    for k in range(3):
        for block in range(nblocks):
            span = pl.ds(block * BLOCK, BLOCK)
            out_ref[:, k, 0, span] = latest[k, block, : rows // 2]
            out_ref[:, k, 1, span] = latest[k, block, rows // 2 :]


def shards(positions, polarizability, applied_field, pair_codes, pair_counts):
    freqs = polarizability.shape[0]
    nblocks = positions.shape[1] // BLOCK
    pairs = pair_codes.shape[0]
    rows = 2 * freqs
    sizes = (lax.axis_size("gx"), lax.axis_size("gy"), nblocks, pairs)
    field = jnp.swapaxes(applied_field, 1, 2)
    vmem = pl.BlockSpec(memory_space=pltpu.VMEM)
    smem = pl.BlockSpec(memory_space=pltpu.SMEM)
    wide = 3 * BLOCK
    dma = pltpu.SemaphoreType.DMA
    out = pl.pallas_call(
        functools.partial(kernel, sizes),
        out_shape=jax.ShapeDtypeStruct(field.shape, jnp.float32),
        in_specs=[smem, smem, vmem, vmem, vmem],
        out_specs=vmem,
        scratch_shapes=[
            pltpu.VMEM((nblocks, rows, BLOCK), jnp.float32),
            pltpu.VMEM((nblocks, rows, BLOCK), jnp.float32),
            pltpu.VMEM((3, nblocks, rows, BLOCK), jnp.float32),
            pltpu.VMEM((3, nblocks, 8, BLOCK), jnp.float32),
            pltpu.VMEM((6, nblocks, 8, BLOCK), jnp.float32),
            pltpu.VMEM((pairs, 3, 2 * BLOCK, 2 * BLOCK), jnp.bfloat16),
            pltpu.VMEM((pairs * rows, 6 * nblocks * rows), jnp.float32),
            pltpu.VMEM((6 * nblocks * rows, pairs * rows), jnp.bfloat16),
            pltpu.VMEM((ITERS, 3, 3, nblocks, rows, BLOCK), jnp.float32),
            pltpu.VMEM((3, nblocks, 6 * rows, BLOCK), jnp.bfloat16),
            pltpu.VMEM((pairs * rows, wide), jnp.float32),
            pltpu.VMEM((3, nblocks, rows, BLOCK), jnp.float32),
            pltpu.VMEM((ITERS, 3, 6, nblocks, rows, BLOCK), jnp.float32),
            pltpu.VMEM((ITERS, 3, 3, nblocks, rows, BLOCK), jnp.float32),
            pltpu.VMEM((ITERS, 3, 2, nblocks, rows, BLOCK), jnp.float32),
            dma((7,)),
            dma((7,)),
            dma((ITERS, 3, 2)),
            dma((ITERS, 3, 2)),
            dma((ITERS, 3)),
            dma((ITERS, 3)),
            dma((ITERS, 3, 2)),
            dma((ITERS, 3, 2)),
        ],
        compiler_params=pltpu.CompilerParams(
            collective_id=0, has_side_effects=True, vmem_limit_bytes=40 * 1024 * 1024
        ),
    )(pair_codes, pair_counts, positions, polarizability, field)
    return jnp.swapaxes(out, 1, 2)


def solution(mesh):
    in_specs = (
        P(None, ("gx", "gy", "gz")),
        P(None, None, ("gx", "gy", "gz")),
        P(None, None, None, ("gx", "gy", "gz")),
        P(("gx", "gy", "gz")),
        P(("gx", "gy", "gz")),
    )
    out_specs = P(None, None, None, ("gx", "gy", "gz"))
    return jax.shard_map(shards, mesh=mesh, in_specs=in_specs, out_specs=out_specs, check_vma=False)
```

```python
import functools
import math

import jax
import jax.numpy as jnp
from jax import lax
from jax.experimental import pallas as pl
from jax.experimental.pallas import tpu as pltpu
from jax.sharding import PartitionSpec as P

BLOCK = 128
ITERS = 4
UNROLL = 8
STRIP = 64

cell_width = 4.0
soften = 1.0
screen = 0.5
coupling = 0.8

CENTER = 0.54
SERIES = (
    0.806488610702616,
    0.7241185361715909,
    0.27511941992319955,
    -0.26086845400919295,
    0.2296813716405795,
    -0.17763507721765817,
    0.1043247007059023,
    -0.02452746718798479,
    -0.07547989643924369,
    0.2975431845822381,
    -0.5276853186117066,
    0.345520543574722,
)
MESH = pl.DeviceIdType.MESH


def split(value):
    high = value.astype(jnp.bfloat16)
    low = (value - high.astype(jnp.float32)).astype(jnp.bfloat16)
    return high, low


def kernel(
    sizes,
    codes_ref,
    count_ref,
    pos_hbm,
    alpha_hbm,
    field_hbm,
    out_ref,
    raw_pos,
    raw_alpha,
    raw_field,
    fetched,
    a1_ref,
    a2_ref,
    field_ref,
    src_pos,
    tgt_pos,
    tensors,
    choose,
    chosen,
    sources,
    halves,
    contribs,
    latest,
    partial,
    depth_in,
    carry_in,
    pos_send,
    pos_recv,
    x_send,
    x_recv,
    z_send,
    z_recv,
    y_send,
    y_recv,
):
    n_x, n_y, nblocks, pairs = sizes
    square = nblocks * nblocks
    rows = field_ref.shape[2]
    x = lax.axis_index("gx")
    y = lax.axis_index("gy")
    z = lax.axis_index("gz")
    x_up, x_down = lax.rem(x + 1, n_x), lax.rem(x + n_x - 1, n_x)
    y_up, y_down = lax.rem(y + 1, n_y), lax.rem(y + n_y - 1, n_y)
    other = 1 - z

    fetches = (
        pltpu.make_async_copy(pos_hbm, raw_pos, fetched.at[0]),
        pltpu.make_async_copy(alpha_hbm, raw_alpha, fetched.at[1]),
        pltpu.make_async_copy(field_hbm, raw_field, fetched.at[2]),
    )
    for fetch in fetches:
        fetch.start()
    barrier = pltpu.get_barrier_semaphore()
    partners = (
        (x_up, y, z),
        (x_down, y, z),
        (x, y_up, z),
        (x, y_down, z),
        (x, y_up, other),
        (x, y_down, other),
        (x, y, other),
    )
    for partner in partners:
        pl.semaphore_signal(barrier, inc=1, device_id=partner, device_id_type=MESH)

    def respond(field, block):
        turned = jnp.concatenate([field[rows // 2 :], field[: rows // 2]], axis=0)
        return a1_ref[block] * field + a2_ref[block] * turned

    src_pos[1] = jnp.zeros_like(src_pos[1])
    for fetch in fetches:
        fetch.wait()
    for block in range(nblocks):
        span = pl.ds(block * BLOCK, BLOCK)
        src_pos[1, block, pl.ds(0, 3), :] = raw_pos[:, span]
        real, imag = raw_alpha[:, 0, span], raw_alpha[:, 1, span]
        a1_ref[block] = jnp.concatenate([real, real], axis=0)
        a2_ref[block] = jnp.concatenate([-imag, imag], axis=0)
        for k in range(3):
            field_ref[k, block] = jnp.concatenate(
                [raw_field[:, k, 0, span], raw_field[:, k, 1, span]], axis=0
            )
    tgt_pos[1] = src_pos[1]
    for k in range(3):
        for block in range(nblocks):
            sources[0, 1, k, block] = respond(field_ref[k, block], block)

    def send(src, dst, send_sem, recv_sem, device):
        return pltpu.make_async_remote_copy(
            src_ref=src,
            dst_ref=dst,
            send_sem=send_sem,
            recv_sem=recv_sem,
            device_id=device,
            device_id_type=MESH,
        )

    pl.semaphore_wait(barrier, len(partners))

    def x_copies(sweep, k):
        own = sources.at[sweep, 1, k]
        return (
            send(own, sources.at[sweep, 0, k], x_send.at[sweep, k, 0], x_recv.at[sweep, k, 0], (x_up, y, z)),
            send(own, sources.at[sweep, 2, k], x_send.at[sweep, k, 1], x_recv.at[sweep, k, 1], (x_down, y, z)),
        )

    pos_copies = (
        send(src_pos.at[1], src_pos.at[0], pos_send.at[0], pos_recv.at[0], (x_up, y, z)),
        send(src_pos.at[1], src_pos.at[2], pos_send.at[1], pos_recv.at[1], (x_down, y, z)),
        send(src_pos.at[1], tgt_pos.at[0], pos_send.at[2], pos_recv.at[2], (x, y_up, z)),
        send(src_pos.at[1], tgt_pos.at[2], pos_send.at[3], pos_recv.at[3], (x, y_down, z)),
        send(src_pos.at[1], tgt_pos.at[3], pos_send.at[4], pos_recv.at[4], (x, y_up, other)),
        send(src_pos.at[1], tgt_pos.at[5], pos_send.at[5], pos_recv.at[5], (x, y_down, other)),
        send(src_pos.at[1], tgt_pos.at[4], pos_send.at[6], pos_recv.at[6], (x, y, other)),
    )
    for copy in pos_copies:
        copy.start()
    for k in range(3):
        for copy in x_copies(0, k):
            copy.start()
    for copy in pos_copies:
        copy.wait()

    def decode(entry):
        code = codes_ref[entry]
        src_block = code % nblocks
        tgt_block = code // nblocks % nblocks
        depth_tgt = code // square % 2
        step_y = code // (2 * square) % 3
        step_x = code // (6 * square)
        turned_depth = (depth_tgt + z) % 2
        return src_block, tgt_block, turned_depth, step_y, step_x

    def build(entry, carried):
        src_block, tgt_block, depth, step_y, step_x = decode(entry)
        src = src_pos[step_x, src_block].T
        tgt = tgt_pos[depth * 3 + step_y, tgt_block]
        shift_x = (step_x - 1).astype(jnp.float32) * -cell_width
        shift_y = (step_y - 1).astype(jnp.float32) * cell_width
        for at in range(0, BLOCK, STRIP):
            strip = slice(at, at + STRIP)
            disp = [
                tgt[0:1] - src[strip, 0:1] + shift_x,
                tgt[1:2] - src[strip, 1:2] + shift_y,
                tgt[2:3] - src[strip, 2:3],
            ]
            dist_sq = disp[0] * disp[0] + disp[1] * disp[1] + disp[2] * disp[2] + soften * soften
            inv = lax.rsqrt(dist_sq)
            inv_sq = inv * inv
            offset = inv - CENTER
            series = jnp.full_like(offset, SERIES[-1])
            for term in SERIES[-2::-1]:
                series = series * offset + term
            scale = jnp.exp(-screen * screen * dist_sq) * inv_sq
            b_term = scale * series
            c_term = scale * (3.0 * inv_sq * series + 2.0 * screen * screen / math.sqrt(math.pi))
            for t in range(3):
                scaled = c_term * disp[t]
                pieces = (scaled * disp[t] - b_term, scaled * disp[(t + 1) % 3])
                for part, value in enumerate(pieces):
                    high, low = split(value)
                    lanes = pl.ds(part * BLOCK, BLOCK)
                    tensors[entry, t, pl.ds(at, STRIP), lanes] = high
                    tensors[entry, t, pl.ds(BLOCK + at, STRIP), lanes] = low
        slot = (depth * 3 + step_y) * nblocks + tgt_block
        slot = jnp.where(entry < count_ref[0], slot, -1)
        shape = (rows, 6 * nblocks * rows)
        column = lax.broadcasted_iota(jnp.int32, shape, 1)
        row = lax.broadcasted_iota(jnp.int32, shape, 0)
        choose[pl.ds(entry * rows, rows), :] = jnp.where(column == slot * rows + row, 1.0, 0.0)
        return carried

    def build_two(group, carried):
        return build(group * 2 + 1, build(group * 2, carried))

    lax.fori_loop(0, pairs // 2, build_two, 0)
    chosen[...] = choose[...].T.astype(jnp.bfloat16)

    def sweep_step(sweep, carried):
        def arrive(k):
            for copy in x_copies(sweep, k):
                copy.wait()
            for step in range(3):
                for block in range(nblocks):
                    high, low = split(sources[sweep, step, k, block])
                    both = jnp.concatenate([high, low], axis=0)
                    halves[step, block, pl.ds(k * 2 * rows, 2 * rows)] = both

        def tile_dot(entry, t, step_x, src_block):
            if t < 2:
                both = halves[step_x, src_block, pl.ds(t * 2 * rows, 4 * rows)]
            else:
                both = jnp.concatenate(
                    [
                        halves[step_x, src_block, pl.ds(4 * rows, 2 * rows)],
                        halves[step_x, src_block, pl.ds(0, 2 * rows)],
                    ],
                    axis=0,
                )
            both = jnp.concatenate([both, both], axis=1)
            result = jnp.dot(both, tensors[entry, t], preferred_element_type=jnp.float32)
            first = result[:rows] + result[rows : 2 * rows]
            second = result[2 * rows : 3 * rows, BLOCK:] + result[3 * rows :, BLOCK:]
            return first[:, :BLOCK] + second, first[:, BLOCK:]

        def early_step(group, carried):
            for member in range(UNROLL):
                entry = group * UNROLL + member
                src_block, _, _, _, step_x = decode(entry)
                to_x, to_y = tile_dot(entry, 0, step_x, src_block)
                place = pl.ds(entry * rows, rows)
                contribs[place, pl.ds(0, BLOCK)] = to_x
                contribs[place, pl.ds(BLOCK, BLOCK)] = to_y
            return carried

        def late_step(group, carried):
            for member in range(UNROLL):
                entry = group * UNROLL + member
                src_block, _, _, _, step_x = decode(entry)
                to_y, from_y = tile_dot(entry, 1, step_x, src_block)
                to_z, to_x = tile_dot(entry, 2, step_x, src_block)
                place = pl.ds(entry * rows, rows)
                lanes = [pl.ds(k * BLOCK, BLOCK) for k in range(3)]
                contribs[place, lanes[0]] = contribs[place, lanes[0]] + to_x
                contribs[place, lanes[1]] = contribs[place, lanes[1]] + to_y
                contribs[place, lanes[2]] = from_y + to_z
            return carried

        arrive(0)
        arrive(1)
        lax.fori_loop(0, pairs // UNROLL, early_step, 0)
        arrive(2)
        lax.fori_loop(0, pairs // UNROLL, late_step, 0)

        z_copies = [
            send(
                partial.at[sweep, k, pl.ds(3, 3)],
                depth_in.at[sweep, k],
                z_send.at[sweep, k],
                z_recv.at[sweep, k],
                (x, y, other),
            )
            for k in range(3)
        ]
        y_copies = [
            (
                send(
                    partial.at[sweep, k, 0],
                    carry_in.at[sweep, k, 0],
                    y_send.at[sweep, k, 0],
                    y_recv.at[sweep, k, 0],
                    (x, y_down, z),
                ),
                send(
                    partial.at[sweep, k, 2],
                    carry_in.at[sweep, k, 1],
                    y_send.at[sweep, k, 1],
                    y_recv.at[sweep, k, 1],
                    (x, y_up, z),
                ),
            )
            for k in range(3)
        ]
        for k in range(3):
            high, low = split(contribs[:, pl.ds(k * BLOCK, BLOCK)])
            both = jnp.concatenate([high, low], axis=1)
            merged = jnp.dot(chosen[...], both, preferred_element_type=jnp.float32)
            merged = merged[:, :BLOCK] + merged[:, BLOCK:]
            partial[sweep, k] = merged.reshape(6, nblocks, rows, BLOCK)
            z_copies[k].start()
        for k in range(3):
            z_copies[k].wait_recv()
            for step, copy in zip((0, 2), y_copies[k]):
                partial[sweep, k, step] = partial[sweep, k, step] + depth_in[sweep, k, step]
                copy.start()
        for k in range(3):
            for copy in y_copies[k]:
                copy.wait_recv()
            for block in range(nblocks):
                total = (
                    partial[sweep, k, 1, block]
                    + depth_in[sweep, k, 1, block]
                    + (carry_in[sweep, k, 0, block] + carry_in[sweep, k, 1, block])
                )
                dipole = respond(field_ref[k, block] + coupling * total, block)
                latest[k, block] = dipole

            @pl.when(sweep < ITERS - 1)
            def _():
                sources[sweep + 1, 1, k] = latest[k]
                for copy in x_copies(sweep + 1, k):
                    copy.start()

        for k in range(3):
            z_copies[k].wait_send()
            for copy in y_copies[k]:
                copy.wait_send()
        return carried

    lax.fori_loop(0, ITERS, sweep_step, 0)
    for k in range(3):
        for block in range(nblocks):
            span = pl.ds(block * BLOCK, BLOCK)
            out_ref[:, k, 0, span] = latest[k, block, : rows // 2]
            out_ref[:, k, 1, span] = latest[k, block, rows // 2 :]


def shards(positions, polarizability, applied_field, pair_codes, pair_counts):
    freqs = polarizability.shape[0]
    nblocks = positions.shape[1] // BLOCK
    pairs = pair_codes.shape[0]
    rows = 2 * freqs
    sizes = (lax.axis_size("gx"), lax.axis_size("gy"), nblocks, pairs)
    field = jnp.swapaxes(applied_field, 1, 2)
    vmem = pl.BlockSpec(memory_space=pltpu.VMEM)
    hbm = pl.BlockSpec(memory_space=pltpu.HBM)
    smem = pl.BlockSpec(memory_space=pltpu.SMEM)
    wide = 3 * BLOCK
    dma = pltpu.SemaphoreType.DMA
    out = pl.pallas_call(
        functools.partial(kernel, sizes),
        out_shape=jax.ShapeDtypeStruct(field.shape, jnp.float32),
        in_specs=[smem, smem, hbm, hbm, hbm],
        out_specs=vmem,
        scratch_shapes=[
            pltpu.VMEM(positions.shape, jnp.float32),
            pltpu.VMEM(polarizability.shape, jnp.float32),
            pltpu.VMEM(field.shape, jnp.float32),
            dma((3,)),
            pltpu.VMEM((nblocks, rows, BLOCK), jnp.float32),
            pltpu.VMEM((nblocks, rows, BLOCK), jnp.float32),
            pltpu.VMEM((3, nblocks, rows, BLOCK), jnp.float32),
            pltpu.VMEM((3, nblocks, 8, BLOCK), jnp.float32),
            pltpu.VMEM((6, nblocks, 8, BLOCK), jnp.float32),
            pltpu.VMEM((pairs, 3, 2 * BLOCK, 2 * BLOCK), jnp.bfloat16),
            pltpu.VMEM((pairs * rows, 6 * nblocks * rows), jnp.float32),
            pltpu.VMEM((6 * nblocks * rows, pairs * rows), jnp.bfloat16),
            pltpu.VMEM((ITERS, 3, 3, nblocks, rows, BLOCK), jnp.float32),
            pltpu.VMEM((3, nblocks, 6 * rows, BLOCK), jnp.bfloat16),
            pltpu.VMEM((pairs * rows, wide), jnp.float32),
            pltpu.VMEM((3, nblocks, rows, BLOCK), jnp.float32),
            pltpu.VMEM((ITERS, 3, 6, nblocks, rows, BLOCK), jnp.float32),
            pltpu.VMEM((ITERS, 3, 3, nblocks, rows, BLOCK), jnp.float32),
            pltpu.VMEM((ITERS, 3, 2, nblocks, rows, BLOCK), jnp.float32),
            dma((7,)),
            dma((7,)),
            dma((ITERS, 3, 2)),
            dma((ITERS, 3, 2)),
            dma((ITERS, 3)),
            dma((ITERS, 3)),
            dma((ITERS, 3, 2)),
            dma((ITERS, 3, 2)),
        ],
        compiler_params=pltpu.CompilerParams(
            collective_id=0, has_side_effects=True, vmem_limit_bytes=64 * 1024 * 1024
        ),
    )(pair_codes, pair_counts, positions, polarizability, field)
    return jnp.swapaxes(out, 1, 2)


def solution(mesh):
    in_specs = (
        P(None, ("gx", "gy", "gz")),
        P(None, None, ("gx", "gy", "gz")),
        P(None, None, None, ("gx", "gy", "gz")),
        P(("gx", "gy", "gz")),
        P(("gx", "gy", "gz")),
    )
    out_specs = P(None, None, None, ("gx", "gy", "gz"))
    return jax.shard_map(shards, mesh=mesh, in_specs=in_specs, out_specs=out_specs, check_vma=False)
```
